512 devices in a mesh: seq: 64 (over z, y), head: 8 (over x, core).
Axes of the slice: x: 4, y: 8, z: 8, core: 2. Of those that a mesh axis runs over, the one named last changes fastest.
Arguments:
- queries: bfloat16 [32768, 4096], P('seq', 'head'), may hold values from -1.796875 to 1.796875
- keys: bfloat16 [32768, 4096], P('seq', 'head'), may hold values from -1.796875 to 1.796875
- values: bfloat16 [32768, 4096], P('seq', 'head'), may hold values from -40 to 40
- out_grad: bfloat16 [32768, 4096], P('seq', 'head'), may hold values from -6 to 6
- gain: float32 [4096], P('head'), may hold values from 0.1 to 1.9
- doc_starts: int32 [25], replicated, may hold values from 0 to 32512, as said below
Outputs:
- query_grad: bfloat16 [32768, 4096], P('seq', 'head')
- key_grad: bfloat16 [32768, 4096], P('seq', 'head')
- value_grad: bfloat16 [32768, 4096], P('seq', 'head')
The draws below stay inside these ranges and needn't reach their ends.
Inputs may be any that keep to these rules, and one draw needn't show every extreme that they name: `doc_starts`: sorted and distinct; the first is 0; every multiple of 8192 is among them; one of the first three quarters of the pack is a single document of 8192 tokens, each of the other quarters holds 8 documents; the last document starts at 32512.
All inputs are finite; a program needn't handle non-finite values.
Results may differ from the reference program's by a relative error of at most 0.0058.
Values sent between devices are 32-bit elements; how exact they have to be, the bound alone decides.
No kernel may reach another device: no remote copies, remote signals or barrier semaphores. Data moves between devices by JAX's collectives and lax.ppermute only.
A program may use at most 128 MiB of HBM per device.

```python
import jax
import jax.numpy as jnp
from jax import lax

HEADS = 32
DH = 128
TOK_DEV = 512
DOCS_PER = 8
TOKENS = 32768
WIDTH = 4096
DOCS = 25


def draw_doc_starts(key, part):
    key = jax.random.fold_in(key, 11)
    quarter = TOKENS // 4
    tail_start = quarter - TOK_DEV // 2
    long_slot = jax.random.randint(jax.random.fold_in(key, 1), (), 0, 3)
    rows = []
    for quarter_index in range(4):
        sub_key = jax.random.fold_in(key, 20 + quarter_index)
        if quarter_index == 3:
            inner = jax.random.choice(sub_key, tail_start - 1, (DOCS_PER - 2,), replace=False) + 1
            cut_points = jnp.concatenate([inner.astype(jnp.int32), jnp.full((1,), tail_start, jnp.int32)])
        else:
            cut_points = jax.random.choice(sub_key, quarter - 1, (DOCS_PER - 1,), replace=False) + 1
        rows.append(jnp.sort(cut_points).astype(jnp.int32) + quarter_index * quarter)
    all_cuts = jnp.stack(rows)
    slots = jnp.arange(4, dtype=jnp.int32)
    all_cuts = jnp.where(slots[:, None] == long_slot, TOKENS, all_cuts)
    starts_base = slots * quarter
    merged = jnp.sort(jnp.concatenate([starts_base, all_cuts.reshape(-1)]))
    return merged[:DOCS].astype(jnp.int32)


def draw_values(key, part):
    key = jax.random.fold_in(key, 5)
    row_key = jax.random.fold_in(key, 1)
    column_key = jax.random.fold_in(key, 2)
    base_key = jax.random.fold_in(key, 3)
    row_spread = jax.random.uniform(row_key, (TOKENS, 1), jnp.float32) - 0.5
    column = jnp.arange(WIDTH, dtype=jnp.float32) / WIDTH
    column_scale = jnp.exp(jnp.log(10.0) * (jax.random.uniform(column_key, (1, WIDTH), jnp.float32) - 0.5) + 0.5 * jnp.log(3.0) * (column[None, :] - 0.5))
    row_scale = jnp.exp(jnp.log(10.0) * row_spread)
    base = jax.random.normal(base_key, (TOKENS, WIDTH), jnp.float32)
    drawn = jnp.clip(base * row_scale * column_scale, -40.0, 40.0)
    return drawn.astype(jnp.bfloat16)


def shard_levels(stream_key, shape, shards, least, largest):
    loudness, own = 1.0, jax.random.fold_in(stream_key, 6)
    for position, shards_of in shards:
        draws = jnp.exp(jax.random.uniform(jax.random.fold_in(own, position), (shards_of,), jnp.float32, least / len(shards), largest / len(shards)))
        loudness = loudness * jnp.repeat(draws, shape[position] // shards_of).reshape([-1 if axis == position else 1 for axis in range(len(shape))])
    return loudness


def normal_values(own_key, dims, scale, most, split=(), kind=jnp.bfloat16):
    values = jax.random.normal(own_key, dims, jnp.float32) * scale
    if len(split) > 0:
        values = shard_levels(own_key, dims, split, -0.22, 0.18) * values
    return jnp.clip(values, min=-most, max=most).astype(kind)


def setup_inputs(seed: int = 0) -> dict:
    key_of = jax.random.split(jax.random.key(seed), 7)
    return {
        "queries": normal_values(key_of[0], (TOKENS, WIDTH), 0.3, 1.796875, ((0, 64), (1, 8))),
        "keys": normal_values(key_of[1], (TOKENS, WIDTH), 0.3, 1.796875, ((0, 64), (1, 8))),
        "values": draw_values(jax.random.fold_in(key_of[6], 71), 0),
        "out_grad": normal_values(key_of[3], (TOKENS, WIDTH), 1.0, 6.0, ((0, 64), (1, 8))),
        "gain": jnp.clip(1.0 + 0.18 * jax.random.normal(key_of[4], (WIDTH,), jnp.float32), 0.1, 1.9),
        "doc_starts": draw_doc_starts(jax.random.fold_in(key_of[6], 71), 0),
    }


EPSILON = 1e-06

def doc_of(doc_starts, positions):
    started = (doc_starts[None, :] <= positions[:, None]).astype(jnp.int32)
    return lax.optimization_barrier(jnp.sum(started, axis=1)).astype(jnp.int32) - 1

def reference(queries, keys, values, out_grad, gain, doc_starts):
    blocks = TOKENS // TOK_DEV

    def pieces(array):
        return array.reshape(blocks, TOK_DEV, HEADS, DH)
    query_blocks = pieces(queries)
    key_blocks = pieces(keys)
    value_blocks = pieces(values)
    grad_blocks = pieces(out_grad)
    first_all = jnp.arange(blocks, dtype=jnp.int32) * TOK_DEV
    within = jnp.arange(TOK_DEV, dtype=jnp.int32)
    causal = within[None, :] <= within[:, None]
    gain_heads = gain.reshape(HEADS, DH).astype(jnp.float32)

    def forward(running, inputs):
        query_block, key_block, value_block, grad_block, first_pos = inputs
        doc_ids = doc_of(doc_starts, first_pos + within)
        after_doc = doc_of(doc_starts, jnp.reshape(first_pos + TOK_DEV, (1,)))[0]
        prefix_bf = running.astype(jnp.bfloat16)
        query_float = query_block.astype(jnp.float32)
        key_float = key_block.astype(jnp.float32)
        value_float = value_block.astype(jnp.float32)
        allowed = causal & (doc_ids[:, None] == doc_ids[None, :])
        scores = jnp.einsum('thd,shd->hts', query_float, key_float)
        masked_scores = jnp.where(allowed[None], scores, 0.0).astype(jnp.bfloat16)
        head_from = (doc_ids == doc_ids[0]).astype(jnp.float32)
        intra_part = jnp.einsum('hts,she->the', masked_scores.astype(jnp.float32), value_float)
        carried = jnp.einsum('thd,hde->the', query_float, prefix_bf.astype(jnp.float32))
        attended = intra_part + head_from[:, None, None] * carried
        scaled = gain_heads * grad_block.astype(jnp.float32)
        sum_squares = lax.optimization_barrier(jnp.sum(attended * attended, axis=(1, 2)))
        sum_cross = lax.optimization_barrier(jnp.sum(attended * scaled, axis=(1, 2)))
        inverse = lax.rsqrt(sum_squares / WIDTH + EPSILON)[:, None, None]
        normed_grad = (scaled * inverse - attended * (inverse * inverse * inverse) * (sum_cross[:, None, None] / WIDTH)).astype(jnp.bfloat16)
        chosen = (doc_ids == after_doc).astype(jnp.float32)
        kv_state = jnp.einsum('shd,she->hde', key_float * chosen[:, None, None], value_float)
        running = jnp.where(after_doc != doc_ids[0], kv_state, running + kv_state)
        return (running, (normed_grad, prefix_bf))
    zeros_state = jnp.zeros((HEADS, DH, DH), jnp.float32)
    final_state, (normed_grads, prefixes) = lax.scan(forward, zeros_state, (query_blocks, key_blocks, value_blocks, grad_blocks, first_all))

    def backward(later_state, inputs):
        query_block, key_block, value_block, normed_grad, prefix_bf, first_pos = inputs
        doc_ids = doc_of(doc_starts, first_pos + within)
        before_doc = doc_of(doc_starts, jnp.reshape(first_pos - 1, (1,)))[0]
        later_float = later_state.astype(jnp.bfloat16).astype(jnp.float32)
        prefix_float = prefix_bf.astype(jnp.float32)
        query_float = query_block.astype(jnp.float32)
        key_float = key_block.astype(jnp.float32)
        value_float = value_block.astype(jnp.float32)
        delta_float = normed_grad.astype(jnp.float32)
        allowed = causal & (doc_ids[:, None] == doc_ids[None, :])
        scores = jnp.einsum('thd,shd->hts', query_float, key_float)
        masked_scores = jnp.where(allowed[None], scores, 0.0).astype(jnp.bfloat16).astype(jnp.float32)
        products = jnp.einsum('the,she->hts', delta_float, value_float)
        masked_products = jnp.where(allowed[None], products, 0.0).astype(jnp.bfloat16).astype(jnp.float32)
        head_from = (doc_ids == doc_ids[0]).astype(jnp.float32)[:, None, None]
        tail_to = (doc_ids == doc_ids[TOK_DEV - 1]).astype(jnp.float32)[:, None, None]
        query_grad = jnp.einsum('hts,shd->thd', masked_products, key_float) + head_from * jnp.einsum('the,hde->thd', delta_float, prefix_float)
        key_grad = jnp.einsum('hts,thd->shd', masked_products, query_float) + tail_to * jnp.einsum('she,hde->shd', value_float, later_float)
        value_grad = jnp.einsum('hts,the->she', masked_scores, delta_float) + tail_to * jnp.einsum('shd,hde->she', key_float, later_float)
        picked = (doc_ids == before_doc).astype(jnp.float32)
        grad_state = jnp.einsum('thd,the->hde', query_float * picked[:, None, None], delta_float)
        later_state = jnp.where(doc_ids[TOK_DEV - 1] != before_doc, grad_state, later_state + grad_state)
        return (later_state, (query_grad.astype(jnp.bfloat16), key_grad.astype(jnp.bfloat16), value_grad.astype(jnp.bfloat16)))
    first_back, grads = lax.scan(backward, zeros_state, (query_blocks, key_blocks, value_blocks, normed_grads, prefixes, first_all), reverse=True)
    return (grads[0].reshape(TOKENS, WIDTH), grads[1].reshape(TOKENS, WIDTH), grads[2].reshape(TOKENS, WIDTH))
```

```python
import functools

import jax
import jax.numpy as jnp
from jax import lax
from jax.experimental import pallas as pl
from jax.experimental.pallas import tpu as pltpu
from jax.sharding import PartitionSpec as P

DH = 128
WIDTH = 4096
EPSILON = 1e-06
QUARTERS = 4
LOADS = 4

F32 = jnp.float32
BF16 = jnp.bfloat16
I32 = jnp.int32


def dot(a, b, contract):
    return lax.dot_general(a, b, ((contract[:1], contract[1:]), ((), ())), preferred_element_type=F32)


def heads_of(array):
    return [slice(h * DH, (h + 1) * DH) for h in range(array.shape[-1] // DH)]


def row_index(rows):
    return lax.broadcasted_iota(I32, (rows, DH), 0)


def kv_kernel(per, starts_hbm, k_hbm, v_hbm, state_ref, bounds_ref, ends_ref, flags_ref, starts, k_buf, v_buf, sems):
    rows, width = k_buf.shape
    step = rows // LOADS
    starts_copy = pltpu.make_async_copy(starts_hbm, starts, sems.at[0])
    starts_copy.start()
    loads = []
    for i in range(LOADS):
        part = pl.ds(i * step, step)
        loads.append(pltpu.make_async_copy(k_hbm.at[part], k_buf.at[part], sems.at[1 + 2 * i]))
        loads.append(pltpu.make_async_copy(v_hbm.at[part], v_buf.at[part], sems.at[2 + 2 * i]))
    for load in loads:
        load.start()
    pos = lax.axis_index("seq")
    first = pos * rows
    quarter_first = (pos // per) * per * rows
    block = quarter_first + rows * lax.broadcasted_iota(I32, (per, DH), 0)
    column = lax.broadcasted_iota(I32, ends_ref.shape, 1)
    starts_copy.wait()
    head_end = jnp.full((4, DH), rows, I32)
    tail_start = jnp.full((4, DH), 0, I32)
    ends = jnp.full(ends_ref.shape, rows, I32)
    yes = jnp.ones((per, DH), F32)
    no = jnp.zeros((per, DH), F32)
    keep_forward, take_forward, keep_backward, take_backward = yes, yes, yes, yes
    for i in range(starts_hbm.shape[0] - 1, -1, -1):
        start = starts[i]
        here = start - first
        head_end = jnp.where(here > 0, jnp.minimum(head_end, here), head_end)
        tail_start = jnp.where(here < rows, jnp.maximum(tail_start, here), tail_start)
        ends = jnp.where(column < here, jnp.minimum(ends, here), ends)
        offset = start - block
        inside = (offset > 0) & (offset < rows)
        keep_forward = jnp.where(inside | (offset == rows), no, keep_forward)
        take_forward = jnp.where(offset == rows, no, take_forward)
        keep_backward = jnp.where(inside | (offset == 0), no, keep_backward)
        take_backward = jnp.where(offset == 0, no, take_backward)
    bounds_ref[0:4] = head_end
    bounds_ref[4:8] = tail_start
    ends_ref[...] = ends
    for i, flag in enumerate((keep_forward, take_forward, keep_backward, take_backward)):
        flags_ref[i] = flag
    half = rows // 2
    for j in range(2):
        for load in loads[j * LOADS : (j + 1) * LOADS]:
            load.wait()
        part = slice(j * half, (j + 1) * half)
        chosen = row_index(half) + j * half >= tail_start[:1]
        for h, cols in enumerate(heads_of(k_buf)):
            k = jnp.where(chosen, k_buf[part, cols], jnp.zeros((), BF16))
            term = dot(k, v_buf[part, cols], (0, 0))
            state_ref[h] = term if j == 0 else state_ref[h] + term


def scan_kernel(backward, flags_ref, x_ref, out_ref):
    count = x_ref.shape[0]
    order = list(range(count))[:: -1 if backward else 1]
    keep, take = (2, 3) if backward else (0, 1)
    running = jnp.zeros(x_ref.shape[1:], F32)
    out_ref[order[0]] = running
    for b, later in zip(order[:-1], order[1:]):
        running = running * flags_ref[keep, b : b + 1] + x_ref[b] * flags_ref[take, b : b + 1]
        out_ref[later] = running


def allowed_mask(ends_ref):
    rows = ends_ref.shape[1]
    row = lax.broadcasted_iota(I32, (rows, rows), 0)
    return (lax.broadcasted_iota(I32, (rows, rows), 1) <= row) & (row < ends_ref[0:1])


def intra_kernel(bounds_ref, ends_ref, q_ref, k_ref, v_ref, g_ref, gain_ref, scores_ref, intra_ref, scaled_ref, head_ref, turned_ref):
    rows = q_ref.shape[0]
    from_head = row_index(rows) < bounds_ref[0:1]
    allowed = allowed_mask(ends_ref)
    for h, cols in enumerate(heads_of(q_ref)):
        scores = dot(q_ref[:, cols], k_ref[:, cols], (1, 1))
        masked = jnp.where(allowed, scores, 0.0).astype(BF16)
        scores_ref[h] = masked
        intra_ref[:, cols] = dot(masked, v_ref[:, cols], (1, 0))
        scaled_ref[:, cols] = gain_ref[:, cols] * g_ref[:, cols].astype(F32)
        head = jnp.where(from_head, q_ref[:, cols], jnp.zeros((), BF16))
        head_ref[:, cols] = head
        turned_ref[h] = head.T


def attend_kernel(head_ref, intra_ref, prefix_ref, scaled_ref, attended_ref, sums_ref):
    rows = head_ref.shape[0]
    squares = jnp.zeros((rows, DH), F32)
    crosses = jnp.zeros((rows, DH), F32)
    for h, cols in enumerate(heads_of(head_ref)):
        attended = intra_ref[:, cols] + dot(head_ref[:, cols], prefix_ref[h].astype(BF16), (1, 0))
        attended_ref[:, cols] = attended
        squares += attended * attended
        crosses += attended * scaled_ref[:, cols]
    parts = rows // DH
    for i in range(parts):
        part = slice(i * DH, (i + 1) * DH)
        square = jnp.sum(squares[part].T, axis=0, keepdims=True)
        cross = jnp.sum(crosses[part].T, axis=0, keepdims=True)
        for to in range(sums_ref.shape[0]):
            sums_ref[to, i : i + 1] = square
            sums_ref[to, parts + i : parts + i + 1] = cross


def grad_kernel(turned_ref, attended_ref, scaled_ref, sums_ref, normed_ref, state_ref):
    rows = attended_ref.shape[0]
    parts = rows // DH
    sums = jnp.sum(sums_ref[...], axis=0)
    inverse = lax.rsqrt(sums[:parts] / WIDTH + EPSILON)
    factor = inverse * inverse * inverse * (sums[parts:] / WIDTH)
    for i in range(parts):
        part = slice(i * DH, (i + 1) * DH)
        inverse_here = jnp.broadcast_to(inverse[i : i + 1], (DH, DH)).T
        factor_here = jnp.broadcast_to(factor[i : i + 1], (DH, DH)).T
        for cols in heads_of(attended_ref):
            normed = scaled_ref[part, cols] * inverse_here - attended_ref[part, cols] * factor_here
            normed_ref[part, cols] = normed.astype(BF16)
    for h, cols in enumerate(heads_of(attended_ref)):
        state_ref[h] = dot(turned_ref[h], normed_ref[:, cols], (1, 0))


def products_kernel(bounds_ref, ends_ref, q_ref, k_ref, v_ref, normed_ref, prefix_ref, scores_ref, dq_ref, dk_ref, dv_ref):
    rows = q_ref.shape[0]
    from_head = row_index(rows) < bounds_ref[0:1]
    allowed = allowed_mask(ends_ref)
    for h, cols in enumerate(heads_of(q_ref)):
        normed = normed_ref[:, cols]
        products = dot(normed, v_ref[:, cols], (1, 1))
        products = jnp.where(allowed, products, 0.0).astype(BF16)
        carried = dot(normed, prefix_ref[h].astype(BF16), (1, 1))
        dq = dot(products, k_ref[:, cols], (1, 0)) + jnp.where(from_head, carried, 0.0)
        dq_ref[:, cols] = dq.astype(BF16)
        dk_ref[:, cols] = dot(products, q_ref[:, cols], (0, 0))
        dv_ref[:, cols] = dot(scores_ref[h], normed, (0, 0))


def final_kernel(bounds_ref, k_ref, v_ref, dk_ref, dv_ref, later_ref, key_hbm, value_hbm, key_buf, value_buf, sems):
    rows = k_ref.shape[0]
    to_tail = row_index(rows) >= bounds_ref[4:5]
    stores = []
    for h, cols in enumerate(heads_of(k_ref)):
        later = later_ref[h].astype(BF16)
        dk = dot(v_ref[:, cols], later, (1, 1))
        key_buf[:, cols] = (dk_ref[:, cols] + jnp.where(to_tail, dk, 0.0)).astype(BF16)
        stores.append(pltpu.make_async_copy(key_buf.at[:, cols], key_hbm.at[:, cols], sems.at[2 * h]))
        stores[-1].start()
        dv = dot(k_ref[:, cols], later, (1, 0))
        value_buf[:, cols] = (dv_ref[:, cols] + jnp.where(to_tail, dv, 0.0)).astype(BF16)
        stores.append(pltpu.make_async_copy(value_buf.at[:, cols], value_hbm.at[:, cols], sems.at[2 * h + 1]))
        stores[-1].start()
    for store in stores:
        store.wait()


HBM = pl.BlockSpec(memory_space=pltpu.HBM)
VMEM = pl.BlockSpec(memory_space=pltpu.VMEM)


def call(kernel, arrays, outs, flops, name, in_specs=None, out_spec=VMEM, scratch=()):
    out_shape = tuple(jax.ShapeDtypeStruct(s, d) for s, d in outs)
    moved = sum(a.size * a.dtype.itemsize for a in arrays) + sum(o.size * o.dtype.itemsize for o in out_shape)
    return pl.pallas_call(
        kernel,
        out_shape=out_shape,
        in_specs=in_specs or [VMEM] * len(arrays),
        out_specs=(out_spec,) * len(outs),
        scratch_shapes=list(scratch),
        compiler_params=pltpu.CompilerParams(vmem_limit_bytes=16 * 1024 * 1024),
        cost_estimate=pl.CostEstimate(flops=flops, bytes_accessed=moved, transcendentals=0),
        name=name,
    )(*arrays)


def on_device(queries, keys, values, out_grad, gain, doc_starts):
    rows, width = queries.shape
    heads = width // DH
    per = lax.axis_size("seq") // QUARTERS
    head_devices = lax.axis_size("head")
    gain_row = gain.reshape(1, width)
    groups = [[g * per + i for i in range(per)] for g in range(QUARTERS)]
    state_shape = (heads, DH, DH)
    pieces = (per, heads * DH // per, DH)
    state_flops = 2 * rows * width * DH
    full_flops = 2 * rows * rows * width
    whole = (rows, width)

    def swap(x):
        return lax.all_to_all(x.reshape(pieces), "seq", 0, 0, axis_index_groups=groups, tiled=True)

    def scan(state, flags, backward):
        (mine,) = call(functools.partial(scan_kernel, backward), (flags, swap(state)), [(pieces, F32)], 0, "state_scan")
        return swap(mine).reshape(state_shape)

    kv_state, bounds, ends, flags = call(
        functools.partial(kv_kernel, per),
        (doc_starts, keys, values),
        [(state_shape, F32), ((8, DH), I32), ((8, rows), I32), ((4, per, DH), F32)],
        state_flops,
        "kv_state",
        in_specs=[HBM] * 3,
        scratch=[
            pltpu.SMEM(doc_starts.shape, I32),
            pltpu.VMEM(whole, BF16),
            pltpu.VMEM(whole, BF16),
            pltpu.SemaphoreType.DMA((1 + 2 * LOADS,)),
        ],
    )
    prefix = scan(kv_state, flags, False)
    scores, intra, scaled, head, turned = call(
        intra_kernel,
        (bounds, ends, queries, keys, values, out_grad, gain_row),
        [((heads, rows, rows), BF16), (whole, F32), (whole, F32), (whole, BF16), ((heads, DH, rows), BF16)],
        2 * full_flops,
        "intra",
    )
    attended, sums = call(
        attend_kernel,
        (head, intra, prefix, scaled),
        [(whole, F32), ((head_devices, 2 * rows // DH, DH), F32)],
        state_flops,
        "attend",
    )
    sums = lax.all_to_all(sums, "head", 0, 0, tiled=True)
    normed, grad_state = call(
        grad_kernel,
        (turned, attended, scaled, sums),
        [(whole, BF16), (state_shape, F32)],
        state_flops,
        "normed_grad",
    )
    later = scan(grad_state, flags, True)
    query_grad, key_part, value_part = call(
        products_kernel,
        (bounds, ends, queries, keys, values, normed, prefix, scores),
        [(whole, BF16), (whole, F32), (whole, F32)],
        4 * full_flops + state_flops,
        "products",
    )
    key_grad, value_grad = call(
        final_kernel,
        (bounds, keys, values, key_part, value_part, later),
        [(whole, BF16), (whole, BF16)],
        2 * state_flops,
        "key_value_grad",
        out_spec=HBM,
        scratch=[
            pltpu.VMEM(whole, BF16),
            pltpu.VMEM(whole, BF16),
            pltpu.SemaphoreType.DMA((2 * heads,)),
        ],
    )
    return query_grad, key_grad, value_grad


def solution(mesh):
    placed = (P("seq", "head"),) * 4 + (P("head"), P())
    return jax.shard_map(
        on_device,
        mesh=mesh,
        in_specs=placed,
        out_specs=(P("seq", "head"),) * 3,
        check_vma=False,
    )
```

```python
import functools

import jax
import jax.numpy as jnp
from jax import lax
from jax.experimental import pallas as pl
from jax.experimental.pallas import tpu as pltpu
from jax.sharding import PartitionSpec as P

DH = 128
WIDTH = 4096
EPSILON = 1e-06
QUARTERS = 4
LOADS = 4

F32 = jnp.float32
BF16 = jnp.bfloat16
I32 = jnp.int32


def dot(a, b, contract):
    return lax.dot_general(a, b, ((contract[:1], contract[1:]), ((), ())), preferred_element_type=F32)


def heads_of(array):
    return [slice(h * DH, (h + 1) * DH) for h in range(array.shape[-1] // DH)]


def row_index(rows):
    return lax.broadcasted_iota(I32, (rows, DH), 0)


def kv_kernel(per, starts_hbm, k_hbm, v_hbm, state_ref, bounds_ref, edges_ref, flags_ref, starts, k_buf, v_buf, sems):
    rows, width = k_buf.shape
    step = rows // LOADS
    starts_copy = pltpu.make_async_copy(starts_hbm, starts, sems.at[0])
    starts_copy.start()
    loads = []
    for i in range(LOADS):
        part = pl.ds(i * step, step)
        loads.append(pltpu.make_async_copy(k_hbm.at[part], k_buf.at[part], sems.at[1 + 2 * i]))
        loads.append(pltpu.make_async_copy(v_hbm.at[part], v_buf.at[part], sems.at[2 + 2 * i]))
    for load in loads:
        load.start()
    pos = lax.axis_index("seq")
    first = pos * rows
    block = (pos // per) * per * rows + rows * lax.broadcasted_iota(I32, (per, DH), 0)
    column = lax.broadcasted_iota(I32, (4, rows), 1)
    head_end = jnp.int32(rows)
    tail = jnp.int32(0)
    begins = jnp.full((4, rows), 0, I32)
    ends = jnp.full((4, rows), rows, I32)
    yes = jnp.ones((per, DH), F32)
    no = jnp.zeros((per, DH), F32)
    keep_forward, take_forward, keep_backward, take_backward = yes, yes, yes, yes
    starts_copy.wait()
    for i in range(starts_hbm.shape[0]):
        start = starts[i]
        here = start - first
        head_end = jnp.where(here > 0, jnp.minimum(head_end, here), head_end)
        tail = jnp.where(here < rows, jnp.maximum(tail, here), tail)
        begins = jnp.where(column >= here, jnp.maximum(begins, here), begins)
        ends = jnp.where(column < here, jnp.minimum(ends, here), ends)
        offset = start - block
        inside = (offset > 0) & (offset < rows)
        keep_forward = jnp.where(inside | (offset == rows), no, keep_forward)
        take_forward = jnp.where(offset == rows, no, take_forward)
        keep_backward = jnp.where(inside | (offset == 0), no, keep_backward)
        take_backward = jnp.where(offset == 0, no, take_backward)
    bounds_ref[0:4] = jnp.full((4, DH), head_end, I32)
    bounds_ref[4:8] = jnp.full((4, DH), tail, I32)
    edges_ref[0:4] = begins
    edges_ref[4:8] = ends
    for i, flag in enumerate((keep_forward, take_forward, keep_backward, take_backward)):
        flags_ref[i] = flag
    for i in range(LOADS):
        loads[2 * i].wait()
        loads[2 * i + 1].wait()
        part = slice(i * step, (i + 1) * step)
        chosen = row_index(step) + i * step >= tail
        for h, cols in enumerate(heads_of(k_buf)):
            k = jnp.where(chosen, k_buf[part, cols], jnp.zeros((), BF16))
            term = dot(k, v_buf[part, cols], (0, 0))
            state_ref[h] = term if i == 0 else state_ref[h] + term


def scan_kernel(backward, flags_ref, x_ref, out_ref):
    count = x_ref.shape[0]
    order = list(range(count))[:: -1 if backward else 1]
    keep, take = (2, 3) if backward else (0, 1)
    running = jnp.zeros(x_ref.shape[1:], F32)
    out_ref[order[0]] = running
    for b, later in zip(order[:-1], order[1:]):
        running = running * flags_ref[keep, b : b + 1] + x_ref[b] * flags_ref[take, b : b + 1]
        out_ref[later] = running


def masked_scores(q, k, ends):
    half = q.shape[0] // 2
    parts = []
    for start, size in ((0, half), (half, 2 * half)):
        token = lax.broadcasted_iota(I32, (half, size), 0) + start
        source = lax.broadcasted_iota(I32, (half, size), 1)
        allowed = (source <= token) & (token < ends[:, :size])
        parts.append(jnp.where(allowed, dot(q[start : start + half], k[:size], (1, 1)), 0.0).astype(BF16))
    return parts


def masked_turned(k, q, begins):
    half = q.shape[0] // 2
    parts = []
    for start, size in ((0, half), (half, 2 * half)):
        token = lax.broadcasted_iota(I32, (size, half), 1) + start
        source = lax.broadcasted_iota(I32, (size, half), 0)
        allowed = (source <= token) & (source >= begins[:, start : start + half])
        parts.append(jnp.where(allowed, dot(k[:size], q[start : start + half], (1, 1)), 0.0).astype(BF16))
    return parts


def intra_kernel(bounds_ref, edges_ref, flags_ref, q_ref, k_ref, v_ref, gain_ref, intra_ref, bounds_out_ref, flags_out_ref, gain_out_ref):
    half = q_ref.shape[0] // 2
    ends = edges_ref[4:5]
    bounds_out_ref[...] = bounds_ref[...]
    flags_out_ref[...] = flags_ref[...]
    gain_out_ref[...] = gain_ref[...]
    for cols in heads_of(q_ref):
        early, late = masked_scores(q_ref[:, cols], k_ref[:, cols], ends)
        intra_ref[:half, cols] = dot(early, v_ref[:half, cols], (1, 0))
        intra_ref[half:, cols] = dot(late, v_ref[:, cols], (1, 0))


def attend_kernel(bounds_ref, q_ref, intra_ref, prefix_ref, g_ref, gain_ref, attended_ref, sums_ref):
    rows = q_ref.shape[0]
    parts = rows // DH
    prefix = [prefix_ref[h].astype(BF16) for h in range(prefix_ref.shape[0])]
    for i in range(parts):
        part = slice(i * DH, (i + 1) * DH)
        from_head = row_index(DH) + i * DH < bounds_ref[0:1]
        squares = jnp.zeros((DH, DH), F32)
        crosses = jnp.zeros((DH, DH), F32)
        for h, cols in enumerate(heads_of(q_ref)):
            carried = dot(q_ref[part, cols], prefix[h], (1, 0))
            attended = intra_ref[part, cols] + jnp.where(from_head, carried, 0.0)
            attended_ref[part, cols] = attended
            squares += attended * attended
            crosses += attended * (gain_ref[:, cols] * g_ref[part, cols].astype(F32))
        square = jnp.sum(squares.T, axis=0, keepdims=True)
        cross = jnp.sum(crosses.T, axis=0, keepdims=True)
        for to in range(sums_ref.shape[0]):
            sums_ref[to, i : i + 1] = square
            sums_ref[to, parts + i : parts + i + 1] = cross


def grad_kernel(bounds_ref, q_ref, attended_ref, g_ref, gain_ref, sums_ref, normed_ref, state_ref):
    rows = attended_ref.shape[0]
    parts = rows // DH
    sums = jnp.sum(sums_ref[...], axis=0)
    inverse = lax.rsqrt(sums[:parts] / WIDTH + EPSILON)
    factor = inverse * inverse * inverse * (sums[parts:] / WIDTH)
    for i in range(parts):
        part = slice(i * DH, (i + 1) * DH)
        from_head = row_index(DH) + i * DH < bounds_ref[0:1]
        inverse_here = jnp.broadcast_to(inverse[i : i + 1], (DH, DH)).T
        factor_here = jnp.broadcast_to(factor[i : i + 1], (DH, DH)).T
        for h, cols in enumerate(heads_of(q_ref)):
            scaled = gain_ref[:, cols] * g_ref[part, cols].astype(F32)
            normed = (scaled * inverse_here - attended_ref[part, cols] * factor_here).astype(BF16)
            normed_ref[part, cols] = normed
            term = dot(jnp.where(from_head, q_ref[part, cols], jnp.zeros((), BF16)), normed, (0, 0))
            state_ref[h] = term if i == 0 else state_ref[h] + term


def products_kernel(
    bounds_ref, edges_ref, q_ref, k_ref, v_ref, normed_ref, prefix_ref, dq_ref, dk_ref, dv_ref
):
    rows = q_ref.shape[0]
    half = rows // 2
    from_head = row_index(rows) < bounds_ref[0:1]
    begins = edges_ref[0:1]
    for h, cols in enumerate(heads_of(q_ref)):
        q, k, normed = q_ref[:, cols], k_ref[:, cols], normed_ref[:, cols]
        early, late = masked_turned(k, q, begins)
        upper = dot(late, normed[half:], (1, 0))
        dv_ref[:half, cols] = (upper[:half] + dot(early, normed[:half], (1, 0))).astype(BF16)
        dv_ref[half:, cols] = upper[half:].astype(BF16)
        early, late = masked_turned(v_ref[:, cols], normed, begins)
        upper = dot(late, q[half:], (1, 0))
        dk_ref[:half, cols] = (upper[:half] + dot(early, q[:half], (1, 0))).astype(BF16)
        dk_ref[half:, cols] = upper[half:].astype(BF16)
        carried = dot(normed, prefix_ref[h].astype(BF16), (1, 1))
        carried = jnp.where(from_head, carried, 0.0)
        dq_ref[:half, cols] = (dot(early, k[:half], (0, 0)) + carried[:half]).astype(BF16)
        dq_ref[half:, cols] = (dot(late, k, (0, 0)) + carried[half:]).astype(BF16)


def final_kernel(bounds_ref, k_ref, v_ref, dk_ref, dv_ref, later_ref, key_hbm, value_hbm, key_buf, value_buf, sems):
    rows = k_ref.shape[0]
    to_tail = row_index(rows) >= bounds_ref[4:5]
    stores = []
    for h, cols in enumerate(heads_of(k_ref)):
        later = later_ref[h].astype(BF16)
        dk = dot(v_ref[:, cols], later, (1, 1))
        key_buf[:, cols] = (dk_ref[:, cols] + jnp.where(to_tail, dk, 0.0)).astype(BF16)
        stores.append(pltpu.make_async_copy(key_buf.at[:, cols], key_hbm.at[:, cols], sems.at[2 * h]))
        stores[-1].start()
        dv = dot(k_ref[:, cols], later, (1, 0))
        value_buf[:, cols] = (dv_ref[:, cols] + jnp.where(to_tail, dv, 0.0)).astype(BF16)
        stores.append(pltpu.make_async_copy(value_buf.at[:, cols], value_hbm.at[:, cols], sems.at[2 * h + 1]))
        stores[-1].start()
    for store in stores:
        store.wait()


HBM = pl.BlockSpec(memory_space=pltpu.HBM)
VMEM = pl.BlockSpec(memory_space=pltpu.VMEM)


def call(kernel, arrays, outs, flops, name, in_specs=None, out_specs=None, scratch=(), room=16):
    out_shape = tuple(jax.ShapeDtypeStruct(s, d) for s, d in outs)
    moved = sum(a.size * a.dtype.itemsize for a in arrays) + sum(o.size * o.dtype.itemsize for o in out_shape)
    return pl.pallas_call(
        kernel,
        out_shape=out_shape,
        in_specs=in_specs or [VMEM] * len(arrays),
        out_specs=out_specs or (VMEM,) * len(outs),
        scratch_shapes=list(scratch),
        compiler_params=pltpu.CompilerParams(vmem_limit_bytes=int(room * 1024 * 1024)),
        cost_estimate=pl.CostEstimate(flops=flops, bytes_accessed=moved, transcendentals=0),
        name=name,
    )(*arrays)


def on_device(queries, keys, values, out_grad, gain, doc_starts):
    rows, width = queries.shape
    heads = width // DH
    per = lax.axis_size("seq") // QUARTERS
    head_devices = lax.axis_size("head")
    gain_row = gain.reshape(1, width)
    groups = [[g * per + i for i in range(per)] for g in range(QUARTERS)]
    state_shape = (heads, DH, DH)
    pieces = (per, heads * DH // per, DH)
    state_flops = 2 * rows * width * DH
    full_flops = 2 * rows * rows * width
    whole = (rows, width)

    def swap(x):
        return lax.all_to_all(x.reshape(pieces), "seq", 0, 0, axis_index_groups=groups, tiled=True)

    def scan(state, flags, backward):
        (mine,) = call(functools.partial(scan_kernel, backward), (flags, swap(state)), [(pieces, F32)], 0, "state_scan")
        return swap(mine).reshape(state_shape)

    kv_state, bounds, edges, flags = call(
        functools.partial(kv_kernel, per),
        (doc_starts, keys, values),
        [(state_shape, F32), ((8, DH), I32), ((8, rows), I32), ((4, per, DH), F32)],
        state_flops,
        "kv_state",
        in_specs=[HBM] * 3,
        room=60,
        scratch=[
            pltpu.SMEM(doc_starts.shape, I32),
            pltpu.VMEM(whole, BF16),
            pltpu.VMEM(whole, BF16),
            pltpu.SemaphoreType.DMA((1 + 2 * LOADS,)),
        ],
    )
    intra, bounds, flags, gain_row = call(
        intra_kernel,
        (bounds, edges, flags, queries, keys, values, gain_row),
        [(whole, F32), (bounds.shape, I32), (flags.shape, F32), (gain_row.shape, F32)],
        2 * full_flops,
        "intra",
    )
    prefix = scan(kv_state, flags, False)
    attended, sums = call(
        attend_kernel,
        (bounds, queries, intra, prefix, out_grad, gain_row),
        [(whole, F32), ((head_devices, 2 * rows // DH, DH), F32)],
        state_flops,
        "attend",
    )
    sums = lax.all_to_all(sums, "head", 0, 0, tiled=True)
    normed, grad_state = call(
        grad_kernel,
        (bounds, queries, attended, out_grad, gain_row, sums),
        [(whole, BF16), (state_shape, F32)],
        state_flops,
        "normed_grad",
    )
    later = scan(grad_state, flags, True)
    query_grad, key_part, value_part = call(
        products_kernel,
        (bounds, edges, queries, keys, values, normed, prefix),
        [(whole, BF16), (whole, BF16), (whole, BF16)],
        5 * full_flops + state_flops,
        "products",
    )
    key_grad, value_grad = call(
        final_kernel,
        (bounds, keys, values, key_part, value_part, later),
        [(whole, BF16), (whole, BF16)],
        2 * state_flops,
        "key_value_grad",
        out_specs=(HBM, HBM),
        scratch=[
            pltpu.VMEM(whole, BF16),
            pltpu.VMEM(whole, BF16),
            pltpu.SemaphoreType.DMA((2 * heads,)),
        ],
    )
    return query_grad, key_grad, value_grad


def solution(mesh):
    placed = (P("seq", "head"),) * 4 + (P("head"), P())
    return jax.shard_map(
        on_device,
        mesh=mesh,
        in_specs=placed,
        out_specs=(P("seq", "head"),) * 3,
        check_vma=False,
    )
```

```python
import functools

import jax
import jax.numpy as jnp
from jax import lax
from jax.experimental import pallas as pl
from jax.experimental.pallas import tpu as pltpu
from jax.sharding import PartitionSpec as P

DH = 128
WIDTH = 4096
EPSILON = 1e-06
QUARTERS = 4
LOADS = 4

F32 = jnp.float32
BF16 = jnp.bfloat16
I32 = jnp.int32


def dot(a, b, contract):
    return lax.dot_general(a, b, ((contract[:1], contract[1:]), ((), ())), preferred_element_type=F32)


def heads_of(array):
    return [slice(h * DH, (h + 1) * DH) for h in range(array.shape[-1] // DH)]


def row_index(rows):
    return lax.broadcasted_iota(I32, (rows, DH), 0)


def kv_kernel(per, starts_hbm, k_hbm, v_hbm, state_ref, bounds_ref, edges_ref, flags_ref, starts, k_buf, v_buf, sems):
    rows, width = k_buf.shape
    step = rows // LOADS
    starts_copy = pltpu.make_async_copy(starts_hbm, starts, sems.at[0])
    starts_copy.start()
    loads = []
    for i in range(LOADS):
        part = pl.ds(i * step, step)
        loads.append(pltpu.make_async_copy(k_hbm.at[part], k_buf.at[part], sems.at[1 + 2 * i]))
        loads.append(pltpu.make_async_copy(v_hbm.at[part], v_buf.at[part], sems.at[2 + 2 * i]))
    for load in loads:
        load.start()
    pos = lax.axis_index("seq")
    first = pos * rows
    block = (pos // per) * per * rows + rows * lax.broadcasted_iota(I32, (per, DH), 0)
    column = lax.broadcasted_iota(I32, (4, rows), 1)
    head_end = jnp.int32(rows)
    tail = jnp.int32(0)
    begins = jnp.full((4, rows), 0, I32)
    ends = jnp.full((4, rows), rows, I32)
    yes = jnp.ones((per, DH), F32)
    no = jnp.zeros((per, DH), F32)
    keep_forward, take_forward, keep_backward, take_backward = yes, yes, yes, yes
    starts_copy.wait()
    for i in range(starts_hbm.shape[0]):
        start = starts[i]
        here = start - first
        head_end = jnp.where(here > 0, jnp.minimum(head_end, here), head_end)
        tail = jnp.where(here < rows, jnp.maximum(tail, here), tail)
        begins = jnp.where(column >= here, jnp.maximum(begins, here), begins)
        ends = jnp.where(column < here, jnp.minimum(ends, here), ends)
        offset = start - block
        inside = (offset > 0) & (offset < rows)
        keep_forward = jnp.where(inside | (offset == rows), no, keep_forward)
        take_forward = jnp.where(offset == rows, no, take_forward)
        keep_backward = jnp.where(inside | (offset == 0), no, keep_backward)
        take_backward = jnp.where(offset == 0, no, take_backward)
    bounds_ref[0:4] = jnp.full((4, DH), head_end, I32)
    bounds_ref[4:8] = jnp.full((4, DH), tail, I32)
    edges_ref[0:4] = begins
    edges_ref[4:8] = ends
    for i, flag in enumerate((keep_forward, take_forward, keep_backward, take_backward)):
        flags_ref[i] = flag
    for i in range(LOADS):
        loads[2 * i].wait()
        loads[2 * i + 1].wait()
        part = slice(i * step, (i + 1) * step)
        chosen = row_index(step) + i * step >= tail
        for h, cols in enumerate(heads_of(k_buf)):
            k = jnp.where(chosen, k_buf[part, cols], jnp.zeros((), BF16))
            term = dot(k, v_buf[part, cols], (0, 0))
            state_ref[h] = term if i == 0 else state_ref[h] + term


def fold_order(per):
    row = per // 2
    ring = [i // 2 if i % 2 == 0 else row - 1 - i // 2 for i in range(row)]
    return [z * row + y for z in range(2) for y in ring]


def scan_kernel(backward, flags_ref, x_ref, out_ref):
    count = x_ref.shape[0]
    order = list(range(count))[:: -1 if backward else 1]
    folded = fold_order(count)
    odd = lax.rem(lax.axis_index("head"), 2) == 1
    place = [jnp.where(odd, folded.index(b), b) for b in range(count)]
    keep, take = (2, 3) if backward else (0, 1)
    running = jnp.zeros(x_ref.shape[1:], F32)
    out_ref[place[order[0]]] = running
    for b, later in zip(order[:-1], order[1:]):
        running = running * flags_ref[keep, b : b + 1] + x_ref[place[b]] * flags_ref[take, b : b + 1]
        out_ref[place[later]] = running


def masked_scores(q, k, ends):
    half = q.shape[0] // 2
    parts = []
    for start, size in ((0, half), (half, 2 * half)):
        token = lax.broadcasted_iota(I32, (half, size), 0) + start
        source = lax.broadcasted_iota(I32, (half, size), 1)
        allowed = (source <= token) & (token < ends[:, :size])
        parts.append(jnp.where(allowed, dot(q[start : start + half], k[:size], (1, 1)), 0.0).astype(BF16))
    return parts


def masked_turned(k, q, begins):
    half = q.shape[0] // 2
    parts = []
    for start, size in ((0, half), (half, 2 * half)):
        token = lax.broadcasted_iota(I32, (size, half), 1) + start
        source = lax.broadcasted_iota(I32, (size, half), 0)
        allowed = (source <= token) & (source >= begins[:, start : start + half])
        parts.append(jnp.where(allowed, dot(k[:size], q[start : start + half], (1, 1)), 0.0).astype(BF16))
    return parts


def intra_kernel(bounds_ref, edges_ref, flags_ref, q_ref, k_ref, v_ref, gain_ref, intra_ref, bounds_out_ref, flags_out_ref, gain_out_ref):
    half = q_ref.shape[0] // 2
    ends = edges_ref[4:5]
    bounds_out_ref[...] = bounds_ref[...]
    flags_out_ref[...] = flags_ref[...]
    gain_out_ref[...] = gain_ref[...]
    for cols in heads_of(q_ref):
        early, late = masked_scores(q_ref[:, cols], k_ref[:, cols], ends)
        intra_ref[:half, cols] = dot(early, v_ref[:half, cols], (1, 0))
        intra_ref[half:, cols] = dot(late, v_ref[:, cols], (1, 0))


def attend_kernel(bounds_ref, q_ref, intra_ref, prefix_ref, g_ref, gain_ref, attended_ref, sums_ref):
    rows = q_ref.shape[0]
    parts = rows // DH
    prefix = [prefix_ref[h].astype(BF16) for h in range(prefix_ref.shape[0])]
    for i in range(parts):
        part = slice(i * DH, (i + 1) * DH)
        from_head = row_index(DH) + i * DH < bounds_ref[0:1]
        squares = jnp.zeros((DH, DH), F32)
        crosses = jnp.zeros((DH, DH), F32)
        for h, cols in enumerate(heads_of(q_ref)):
            carried = dot(q_ref[part, cols], prefix[h], (1, 0))
            attended = intra_ref[part, cols] + jnp.where(from_head, carried, 0.0)
            attended_ref[part, cols] = attended
            squares += attended * attended
            crosses += attended * (gain_ref[:, cols] * g_ref[part, cols].astype(F32))
        square = jnp.sum(squares.T, axis=0, keepdims=True)
        cross = jnp.sum(crosses.T, axis=0, keepdims=True)
        for to in range(sums_ref.shape[0]):
            sums_ref[to, i : i + 1] = square
            sums_ref[to, parts + i : parts + i + 1] = cross


def grad_kernel(bounds_ref, q_ref, attended_ref, g_ref, gain_ref, sums_ref, normed_ref, state_ref):
    rows = attended_ref.shape[0]
    parts = rows // DH
    sums = jnp.sum(sums_ref[...], axis=0)
    inverse = lax.rsqrt(sums[:parts] / WIDTH + EPSILON)
    factor = inverse * inverse * inverse * (sums[parts:] / WIDTH)
    for i in range(parts):
        part = slice(i * DH, (i + 1) * DH)
        from_head = row_index(DH) + i * DH < bounds_ref[0:1]
        inverse_here = jnp.broadcast_to(inverse[i : i + 1], (DH, DH)).T
        factor_here = jnp.broadcast_to(factor[i : i + 1], (DH, DH)).T
        for h, cols in enumerate(heads_of(q_ref)):
            scaled = gain_ref[:, cols] * g_ref[part, cols].astype(F32)
            normed = (scaled * inverse_here - attended_ref[part, cols] * factor_here).astype(BF16)
            normed_ref[part, cols] = normed
            term = dot(jnp.where(from_head, q_ref[part, cols], jnp.zeros((), BF16)), normed, (0, 0))
            state_ref[h] = term if i == 0 else state_ref[h] + term


def products_kernel(
    bounds_ref, edges_ref, q_ref, k_ref, v_ref, normed_ref, prefix_ref, dq_ref, dk_ref, dv_ref
):
    rows = q_ref.shape[0]
    half = rows // 2
    from_head = row_index(rows) < bounds_ref[0:1]
    begins = edges_ref[0:1]
    for h, cols in enumerate(heads_of(q_ref)):
        q, k, normed = q_ref[:, cols], k_ref[:, cols], normed_ref[:, cols]
        early, late = masked_turned(k, q, begins)
        upper = dot(late, normed[half:], (1, 0))
        dv_ref[:half, cols] = (upper[:half] + dot(early, normed[:half], (1, 0))).astype(BF16)
        dv_ref[half:, cols] = upper[half:].astype(BF16)
        early, late = masked_turned(v_ref[:, cols], normed, begins)
        upper = dot(late, q[half:], (1, 0))
        dk_ref[:half, cols] = (upper[:half] + dot(early, q[:half], (1, 0))).astype(BF16)
        dk_ref[half:, cols] = upper[half:].astype(BF16)
        carried = dot(normed, prefix_ref[h].astype(BF16), (1, 1))
        carried = jnp.where(from_head, carried, 0.0)
        dq_ref[:half, cols] = (dot(early, k[:half], (0, 0)) + carried[:half]).astype(BF16)
        dq_ref[half:, cols] = (dot(late, k, (0, 0)) + carried[half:]).astype(BF16)


def final_kernel(bounds_ref, k_ref, v_ref, dk_ref, dv_ref, later_ref, key_hbm, value_hbm, key_buf, value_buf, sems):
    rows = k_ref.shape[0]
    to_tail = row_index(rows) >= bounds_ref[4:5]
    stores = []
    for h, cols in enumerate(heads_of(k_ref)):
        later = later_ref[h].astype(BF16)
        dk = dot(v_ref[:, cols], later, (1, 1))
        key_buf[:, cols] = (dk_ref[:, cols] + jnp.where(to_tail, dk, 0.0)).astype(BF16)
        stores.append(pltpu.make_async_copy(key_buf.at[:, cols], key_hbm.at[:, cols], sems.at[2 * h]))
        stores[-1].start()
        dv = dot(k_ref[:, cols], later, (1, 0))
        value_buf[:, cols] = (dv_ref[:, cols] + jnp.where(to_tail, dv, 0.0)).astype(BF16)
        stores.append(pltpu.make_async_copy(value_buf.at[:, cols], value_hbm.at[:, cols], sems.at[2 * h + 1]))
        stores[-1].start()
    for store in stores:
        store.wait()


HBM = pl.BlockSpec(memory_space=pltpu.HBM)
VMEM = pl.BlockSpec(memory_space=pltpu.VMEM)


def call(kernel, arrays, outs, flops, name, in_specs=None, out_specs=None, scratch=(), room=16):
    out_shape = tuple(jax.ShapeDtypeStruct(s, d) for s, d in outs)
    moved = sum(a.size * a.dtype.itemsize for a in arrays) + sum(o.size * o.dtype.itemsize for o in out_shape)
    return pl.pallas_call(
        kernel,
        out_shape=out_shape,
        in_specs=in_specs or [VMEM] * len(arrays),
        out_specs=out_specs or (VMEM,) * len(outs),
        scratch_shapes=list(scratch),
        compiler_params=pltpu.CompilerParams(vmem_limit_bytes=int(room * 1024 * 1024)),
        cost_estimate=pl.CostEstimate(flops=flops, bytes_accessed=moved, transcendentals=0),
        name=name,
    )(*arrays)


def on_device(queries, keys, values, out_grad, gain, doc_starts):
    rows, width = queries.shape
    heads = width // DH
    per = lax.axis_size("seq") // QUARTERS
    head_devices = lax.axis_size("head")
    gain_row = gain.reshape(1, width)
    orders = (list(range(per)), fold_order(per))
    groups = [
        [(g * per + b) * head_devices + m for b in orders[m % 2]] for g in range(QUARTERS) for m in range(head_devices)
    ]
    state_shape = (heads, DH, DH)
    pieces = (per, heads * DH // per, DH)
    state_flops = 2 * rows * width * DH
    full_flops = 2 * rows * rows * width
    whole = (rows, width)

    def swap(x):
        return lax.all_to_all(x.reshape(pieces), ("seq", "head"), 0, 0, axis_index_groups=groups, tiled=True)

    def scan(state, flags, backward):
        (mine,) = call(functools.partial(scan_kernel, backward), (flags, swap(state)), [(pieces, F32)], 0, "state_scan")
        return swap(mine).reshape(state_shape)

    kv_state, bounds, edges, flags = call(
        functools.partial(kv_kernel, per),
        (doc_starts, keys, values),
        [(state_shape, F32), ((8, DH), I32), ((8, rows), I32), ((4, per, DH), F32)],
        state_flops,
        "kv_state",
        in_specs=[HBM] * 3,
        room=60,
        scratch=[
            pltpu.SMEM(doc_starts.shape, I32),
            pltpu.VMEM(whole, BF16),
            pltpu.VMEM(whole, BF16),
            pltpu.SemaphoreType.DMA((1 + 2 * LOADS,)),
        ],
    )
    intra, bounds, flags, gain_row = call(
        intra_kernel,
        (bounds, edges, flags, queries, keys, values, gain_row),
        [(whole, F32), (bounds.shape, I32), (flags.shape, F32), (gain_row.shape, F32)],
        2 * full_flops,
        "intra",
    )
    prefix = scan(kv_state, flags, False)
    attended, sums = call(
        attend_kernel,
        (bounds, queries, intra, prefix, out_grad, gain_row),
        [(whole, F32), ((head_devices, 2 * rows // DH, DH), F32)],
        state_flops,
        "attend",
    )
    sums = lax.all_to_all(sums, "head", 0, 0, tiled=True)
    normed, grad_state = call(
        grad_kernel,
        (bounds, queries, attended, out_grad, gain_row, sums),
        [(whole, BF16), (state_shape, F32)],
        state_flops,
        "normed_grad",
    )
    later = scan(grad_state, flags, True)
    query_grad, key_part, value_part = call(
        products_kernel,
        (bounds, edges, queries, keys, values, normed, prefix),
        [(whole, BF16), (whole, BF16), (whole, BF16)],
        5 * full_flops + state_flops,
        "products",
    )
    key_grad, value_grad = call(
        final_kernel,
        (bounds, keys, values, key_part, value_part, later),
        [(whole, BF16), (whole, BF16)],
        2 * state_flops,
        "key_value_grad",
        out_specs=(HBM, HBM),
        scratch=[
            pltpu.VMEM(whole, BF16),
            pltpu.VMEM(whole, BF16),
            pltpu.SemaphoreType.DMA((2 * heads,)),
        ],
    )
    return query_grad, key_grad, value_grad


def solution(mesh):
    placed = (P("seq", "head"),) * 4 + (P("head"), P())
    return jax.shard_map(
        on_device,
        mesh=mesh,
        in_specs=placed,
        out_specs=(P("seq", "head"),) * 3,
        check_vma=False,
    )
```

```python
import functools

import jax
import jax.numpy as jnp
from jax import lax
from jax.experimental import pallas as pl
from jax.experimental.pallas import tpu as pltpu
from jax.sharding import PartitionSpec as P

DH = 128
WIDTH = 4096
EPSILON = 1e-06
QUARTERS = 4
LOADS = 4

F32 = jnp.float32
BF16 = jnp.bfloat16
I32 = jnp.int32


def dot(a, b, contract):
    return lax.dot_general(a, b, ((contract[:1], contract[1:]), ((), ())), preferred_element_type=F32)


def heads_of(array):
    return [slice(h * DH, (h + 1) * DH) for h in range(array.shape[-1] // DH)]


def row_index(rows):
    return lax.broadcasted_iota(I32, (rows, DH), 0)


def kv_kernel(per, starts_hbm, k_hbm, v_hbm, state_ref, bounds_ref, edges_ref, flags_ref, starts, k_buf, v_buf, sems):
    rows, width = k_buf.shape
    step = rows // LOADS
    starts_copy = pltpu.make_async_copy(starts_hbm, starts, sems.at[0])
    starts_copy.start()
    loads = []
    for i in range(LOADS):
        part = pl.ds(i * step, step)
        loads.append(pltpu.make_async_copy(k_hbm.at[part], k_buf.at[part], sems.at[1 + 2 * i]))
        loads.append(pltpu.make_async_copy(v_hbm.at[part], v_buf.at[part], sems.at[2 + 2 * i]))
    for load in loads:
        load.start()
    pos = lax.axis_index("seq")
    first = pos * rows
    block = (pos // per) * per * rows + rows * lax.broadcasted_iota(I32, (per, DH), 0)
    column = lax.broadcasted_iota(I32, (4, rows), 1)
    head_end = jnp.int32(rows)
    tail = jnp.int32(0)
    begins = jnp.full((4, rows), 0, I32)
    ends = jnp.full((4, rows), rows, I32)
    yes = jnp.ones((per, DH), F32)
    no = jnp.zeros((per, DH), F32)
    keep_forward, take_forward, keep_backward, take_backward = yes, yes, yes, yes
    starts_copy.wait()
    for i in range(starts_hbm.shape[0]):
        start = starts[i]
        here = start - first
        head_end = jnp.where(here > 0, jnp.minimum(head_end, here), head_end)
        tail = jnp.where(here < rows, jnp.maximum(tail, here), tail)
        begins = jnp.where(column >= here, jnp.maximum(begins, here), begins)
        ends = jnp.where(column < here, jnp.minimum(ends, here), ends)
        offset = start - block
        inside = (offset > 0) & (offset < rows)
        keep_forward = jnp.where(inside | (offset == rows), no, keep_forward)
        take_forward = jnp.where(offset == rows, no, take_forward)
        keep_backward = jnp.where(inside | (offset == 0), no, keep_backward)
        take_backward = jnp.where(offset == 0, no, take_backward)
    bounds_ref[0:4] = jnp.full((4, DH), head_end, I32)
    bounds_ref[4:8] = jnp.full((4, DH), tail, I32)
    edges_ref[0:4] = begins
    edges_ref[4:8] = ends
    for i, flag in enumerate((keep_forward, take_forward, keep_backward, take_backward)):
        flags_ref[i] = flag
    for i in range(LOADS):
        loads[2 * i].wait()
        loads[2 * i + 1].wait()
        part = slice(i * step, (i + 1) * step)
        chosen = row_index(step) + i * step >= tail
        for h, cols in enumerate(heads_of(k_buf)):
            k = jnp.where(chosen, k_buf[part, cols], jnp.zeros((), BF16))
            term = dot(k, v_buf[part, cols], (0, 0))
            state_ref[h] = term if i == 0 else state_ref[h] + term


def block_orders(per, backward):
    ring = per // 2
    plain = list(range(per))
    fold = [i // 2 if i % 2 == 0 else ring - 1 - i // 2 for i in range(ring)]
    folded = [z * ring + y for z in range(2) for y in fold]
    return plain, folded if backward else folded[ring:] + folded[:ring]


def scan_kernel(backward, flags_ref, x_ref, out_ref):
    count = x_ref.shape[0]
    order = list(range(count))[:: -1 if backward else 1]
    even_order, odd_order = block_orders(count, backward)
    odd = lax.rem(lax.axis_index("head"), 2) == 1
    place = [jnp.where(odd, odd_order.index(b), even_order.index(b)) for b in range(count)]
    keep, take = (2, 3) if backward else (0, 1)
    running = jnp.zeros(x_ref.shape[1:], F32)
    out_ref[place[order[0]]] = running
    for b, later in zip(order[:-1], order[1:]):
        running = running * flags_ref[keep, b : b + 1] + x_ref[place[b]] * flags_ref[take, b : b + 1]
        out_ref[place[later]] = running


def masked_scores(q, k, ends):
    half = q.shape[0] // 2
    parts = []
    for start, size in ((0, half), (half, 2 * half)):
        token = lax.broadcasted_iota(I32, (half, size), 0) + start
        source = lax.broadcasted_iota(I32, (half, size), 1)
        allowed = (source <= token) & (token < ends[:, :size])
        parts.append(jnp.where(allowed, dot(q[start : start + half], k[:size], (1, 1)), 0.0).astype(BF16))
    return parts


def masked_turned(k, q, begins):
    half = q.shape[0] // 2
    parts = []
    for start, size in ((0, half), (half, 2 * half)):
        token = lax.broadcasted_iota(I32, (size, half), 1) + start
        source = lax.broadcasted_iota(I32, (size, half), 0)
        allowed = (source <= token) & (source >= begins[:, start : start + half])
        parts.append(jnp.where(allowed, dot(k[:size], q[start : start + half], (1, 1)), 0.0).astype(BF16))
    return parts


def intra_kernel(bounds_ref, edges_ref, flags_ref, q_ref, k_ref, v_ref, gain_ref, intra_ref, bounds_out_ref, flags_out_ref, gain_out_ref):
    half = q_ref.shape[0] // 2
    ends = edges_ref[4:5]
    bounds_out_ref[...] = bounds_ref[...]
    flags_out_ref[...] = flags_ref[...]
    gain_out_ref[...] = gain_ref[...]
    for cols in heads_of(q_ref):
        early, late = masked_scores(q_ref[:, cols], k_ref[:, cols], ends)
        intra_ref[:half, cols] = dot(early, v_ref[:half, cols], (1, 0))
        intra_ref[half:, cols] = dot(late, v_ref[:, cols], (1, 0))


def attend_kernel(bounds_ref, q_ref, intra_ref, prefix_ref, g_ref, gain_ref, attended_ref, sums_ref):
    rows = q_ref.shape[0]
    parts = rows // DH
    prefix = [prefix_ref[h].astype(BF16) for h in range(prefix_ref.shape[0])]
    for i in range(parts):
        part = slice(i * DH, (i + 1) * DH)
        from_head = row_index(DH) + i * DH < bounds_ref[0:1]
        squares = jnp.zeros((DH, DH), F32)
        crosses = jnp.zeros((DH, DH), F32)
        for h, cols in enumerate(heads_of(q_ref)):
            carried = dot(q_ref[part, cols], prefix[h], (1, 0))
            attended = intra_ref[part, cols] + jnp.where(from_head, carried, 0.0)
            attended_ref[part, cols] = attended
            squares += attended * attended
            crosses += attended * (gain_ref[:, cols] * g_ref[part, cols].astype(F32))
        square = jnp.sum(squares.T, axis=0, keepdims=True)
        cross = jnp.sum(crosses.T, axis=0, keepdims=True)
        for to in range(sums_ref.shape[0]):
            sums_ref[to, i : i + 1] = square
            sums_ref[to, parts + i : parts + i + 1] = cross


def grad_kernel(bounds_ref, q_ref, attended_ref, g_ref, gain_ref, sums_ref, normed_ref, state_ref):
    rows = attended_ref.shape[0]
    parts = rows // DH
    sums = jnp.sum(sums_ref[...], axis=0)
    inverse = lax.rsqrt(sums[:parts] / WIDTH + EPSILON)
    factor = inverse * inverse * inverse * (sums[parts:] / WIDTH)
    for i in range(parts):
        part = slice(i * DH, (i + 1) * DH)
        from_head = row_index(DH) + i * DH < bounds_ref[0:1]
        inverse_here = jnp.broadcast_to(inverse[i : i + 1], (DH, DH)).T
        factor_here = jnp.broadcast_to(factor[i : i + 1], (DH, DH)).T
        for h, cols in enumerate(heads_of(q_ref)):
            scaled = gain_ref[:, cols] * g_ref[part, cols].astype(F32)
            normed = (scaled * inverse_here - attended_ref[part, cols] * factor_here).astype(BF16)
            normed_ref[part, cols] = normed
            term = dot(jnp.where(from_head, q_ref[part, cols], jnp.zeros((), BF16)), normed, (0, 0))
            state_ref[h] = term if i == 0 else state_ref[h] + term


def products_kernel(
    bounds_ref, edges_ref, q_ref, k_ref, v_ref, normed_ref, prefix_ref, dq_ref, dk_ref, dv_ref
):
    rows = q_ref.shape[0]
    half = rows // 2
    from_head = row_index(rows) < bounds_ref[0:1]
    begins = edges_ref[0:1]
    for h, cols in enumerate(heads_of(q_ref)):
        q, k, normed = q_ref[:, cols], k_ref[:, cols], normed_ref[:, cols]
        early, late = masked_turned(k, q, begins)
        upper = dot(late, normed[half:], (1, 0))
        dv_ref[:half, cols] = (upper[:half] + dot(early, normed[:half], (1, 0))).astype(BF16)
        dv_ref[half:, cols] = upper[half:].astype(BF16)
        early, late = masked_turned(v_ref[:, cols], normed, begins)
        upper = dot(late, q[half:], (1, 0))
        dk_ref[:half, cols] = (upper[:half] + dot(early, q[:half], (1, 0))).astype(BF16)
        dk_ref[half:, cols] = upper[half:].astype(BF16)
        carried = dot(normed, prefix_ref[h].astype(BF16), (1, 1))
        carried = jnp.where(from_head, carried, 0.0)
        dq_ref[:half, cols] = (dot(early, k[:half], (0, 0)) + carried[:half]).astype(BF16)
        dq_ref[half:, cols] = (dot(late, k, (0, 0)) + carried[half:]).astype(BF16)


def final_kernel(bounds_ref, k_ref, v_ref, dk_ref, dv_ref, later_ref, key_hbm, value_hbm, key_buf, value_buf, sems):
    rows = k_ref.shape[0]
    to_tail = row_index(rows) >= bounds_ref[4:5]
    stores = []
    for h, cols in enumerate(heads_of(k_ref)):
        later = later_ref[h].astype(BF16)
        dk = dot(v_ref[:, cols], later, (1, 1))
        key_buf[:, cols] = (dk_ref[:, cols] + jnp.where(to_tail, dk, 0.0)).astype(BF16)
        stores.append(pltpu.make_async_copy(key_buf.at[:, cols], key_hbm.at[:, cols], sems.at[2 * h]))
        stores[-1].start()
        dv = dot(k_ref[:, cols], later, (1, 0))
        value_buf[:, cols] = (dv_ref[:, cols] + jnp.where(to_tail, dv, 0.0)).astype(BF16)
        stores.append(pltpu.make_async_copy(value_buf.at[:, cols], value_hbm.at[:, cols], sems.at[2 * h + 1]))
        stores[-1].start()
    for store in stores:
        store.wait()


HBM = pl.BlockSpec(memory_space=pltpu.HBM)
VMEM = pl.BlockSpec(memory_space=pltpu.VMEM)


def call(kernel, arrays, outs, flops, name, in_specs=None, out_specs=None, scratch=(), room=16):
    out_shape = tuple(jax.ShapeDtypeStruct(s, d) for s, d in outs)
    moved = sum(a.size * a.dtype.itemsize for a in arrays) + sum(o.size * o.dtype.itemsize for o in out_shape)
    return pl.pallas_call(
        kernel,
        out_shape=out_shape,
        in_specs=in_specs or [VMEM] * len(arrays),
        out_specs=out_specs or (VMEM,) * len(outs),
        scratch_shapes=list(scratch),
        compiler_params=pltpu.CompilerParams(vmem_limit_bytes=int(room * 1024 * 1024)),
        cost_estimate=pl.CostEstimate(flops=flops, bytes_accessed=moved, transcendentals=0),
        name=name,
    )(*arrays)


def on_device(queries, keys, values, out_grad, gain, doc_starts):
    rows, width = queries.shape
    heads = width // DH
    per = lax.axis_size("seq") // QUARTERS
    head_devices = lax.axis_size("head")
    gain_row = gain.reshape(1, width)
    all_groups = []
    for backward in (False, True):
        orders = block_orders(per, backward)
        all_groups.append(
            [[(g * per + b) * head_devices + m for b in orders[m % 2]] for g in range(QUARTERS) for m in range(head_devices)]
        )
    state_shape = (heads, DH, DH)
    pieces = (per, heads * DH // per, DH)
    state_flops = 2 * rows * width * DH
    full_flops = 2 * rows * rows * width
    whole = (rows, width)

    def swap(x, backward):
        groups = all_groups[backward]
        return lax.all_to_all(x.reshape(pieces), ("seq", "head"), 0, 0, axis_index_groups=groups, tiled=True)

    def scan(state, flags, backward):
        (mine,) = call(functools.partial(scan_kernel, backward), (flags, swap(state, backward)), [(pieces, F32)], 0, "state_scan")
        return swap(mine, backward).reshape(state_shape)

    kv_state, bounds, edges, flags = call(
        functools.partial(kv_kernel, per),
        (doc_starts, keys, values),
        [(state_shape, F32), ((8, DH), I32), ((8, rows), I32), ((4, per, DH), F32)],
        state_flops,
        "kv_state",
        in_specs=[HBM] * 3,
        room=60,
        scratch=[
            pltpu.SMEM(doc_starts.shape, I32),
            pltpu.VMEM(whole, BF16),
            pltpu.VMEM(whole, BF16),
            pltpu.SemaphoreType.DMA((1 + 2 * LOADS,)),
        ],
    )
    intra, bounds, flags, gain_row = call(
        intra_kernel,
        (bounds, edges, flags, queries, keys, values, gain_row),
        [(whole, F32), (bounds.shape, I32), (flags.shape, F32), (gain_row.shape, F32)],
        2 * full_flops,
        "intra",
    )
    prefix = scan(kv_state, flags, False)
    attended, sums = call(
        attend_kernel,
        (bounds, queries, intra, prefix, out_grad, gain_row),
        [(whole, F32), ((head_devices, 2 * rows // DH, DH), F32)],
        state_flops,
        "attend",
    )
    sums = lax.all_to_all(sums, "head", 0, 0, tiled=True)
    normed, grad_state = call(
        grad_kernel,
        (bounds, queries, attended, out_grad, gain_row, sums),
        [(whole, BF16), (state_shape, F32)],
        state_flops,
        "normed_grad",
    )
    later = scan(grad_state, flags, True)
    query_grad, key_part, value_part = call(
        products_kernel,
        (bounds, edges, queries, keys, values, normed, prefix),
        [(whole, BF16), (whole, BF16), (whole, BF16)],
        5 * full_flops + state_flops,
        "products",
    )
    key_grad, value_grad = call(
        final_kernel,
        (bounds, keys, values, key_part, value_part, later),
        [(whole, BF16), (whole, BF16)],
        2 * state_flops,
        "key_value_grad",
        out_specs=(HBM, HBM),
        scratch=[
            pltpu.VMEM(whole, BF16),
            pltpu.VMEM(whole, BF16),
            pltpu.SemaphoreType.DMA((2 * heads,)),
        ],
    )
    return query_grad, key_grad, value_grad


def solution(mesh):
    placed = (P("seq", "head"),) * 4 + (P("head"), P())
    return jax.shard_map(
        on_device,
        mesh=mesh,
        in_specs=placed,
        out_specs=(P("seq", "head"),) * 3,
        check_vma=False,
    )
```

```python
import functools

import jax
import jax.numpy as jnp
from jax import lax
from jax.experimental import pallas as pl
from jax.experimental.pallas import tpu as pltpu
from jax.sharding import PartitionSpec as P

DH = 128
WIDTH = 4096
EPSILON = 1e-06
QUARTERS = 4
LOADS = 1

F32 = jnp.float32
BF16 = jnp.bfloat16
I32 = jnp.int32


def dot(a, b, contract):
    return lax.dot_general(a, b, ((contract[:1], contract[1:]), ((), ())), preferred_element_type=F32)


def heads_of(array):
    return [slice(h * DH, (h + 1) * DH) for h in range(array.shape[-1] // DH)]


def row_index(rows):
    return lax.broadcasted_iota(I32, (rows, DH), 0)


def kv_kernel(per, starts_hbm, k_hbm, v_hbm, state_ref, bounds_ref, edges_ref, flags_ref, starts, k_buf, v_buf, sems):
    rows, width = k_buf.shape
    step = rows // LOADS
    starts_copy = pltpu.make_async_copy(starts_hbm, starts, sems.at[0])
    starts_copy.start()
    loads = []
    for i in range(LOADS):
        part = pl.ds(i * step, step)
        loads.append(pltpu.make_async_copy(k_hbm.at[part], k_buf.at[part], sems.at[1 + 2 * i]))
        loads.append(pltpu.make_async_copy(v_hbm.at[part], v_buf.at[part], sems.at[2 + 2 * i]))
    for load in loads:
        load.start()
    pos = lax.axis_index("seq")
    first = pos * rows
    block = (pos // per) * per * rows + rows * lax.broadcasted_iota(I32, (per, DH), 0)
    column = lax.broadcasted_iota(I32, (4, rows), 1)
    head_end = jnp.int32(rows)
    tail = jnp.int32(0)
    begins = jnp.full((4, rows), 0, I32)
    ends = jnp.full((4, rows), rows, I32)
    yes = jnp.ones((per, DH), F32)
    no = jnp.zeros((per, DH), F32)
    keep_forward, take_forward, keep_backward, take_backward = yes, yes, yes, yes
    starts_copy.wait()
    for i in range(starts_hbm.shape[0]):
        start = starts[i]
        here = start - first
        head_end = jnp.where(here > 0, jnp.minimum(head_end, here), head_end)
        tail = jnp.where(here < rows, jnp.maximum(tail, here), tail)
        begins = jnp.where(column >= here, jnp.maximum(begins, here), begins)
        ends = jnp.where(column < here, jnp.minimum(ends, here), ends)
        offset = start - block
        inside = (offset > 0) & (offset < rows)
        keep_forward = jnp.where(inside | (offset == rows), no, keep_forward)
        take_forward = jnp.where(offset == rows, no, take_forward)
        keep_backward = jnp.where(inside | (offset == 0), no, keep_backward)
        take_backward = jnp.where(offset == 0, no, take_backward)
    bounds_ref[0:4] = jnp.full((4, DH), head_end, I32)
    bounds_ref[4:8] = jnp.full((4, DH), tail, I32)
    edges_ref[0:4] = begins
    edges_ref[4:8] = ends
    for i, flag in enumerate((keep_forward, take_forward, keep_backward, take_backward)):
        flags_ref[i] = flag
    for i in range(LOADS):
        loads[2 * i].wait()
        loads[2 * i + 1].wait()
        part = slice(i * step, (i + 1) * step)
        chosen = row_index(step) + i * step >= tail
        for h, cols in enumerate(heads_of(k_buf)):
            k = jnp.where(chosen, k_buf[part, cols], jnp.zeros((), BF16))
            term = dot(k, v_buf[part, cols], (0, 0))
            state_ref[h] = term if i == 0 else state_ref[h] + term


def block_orders(per, backward):
    ring = per // 2
    plain = list(range(per))
    fold = [i // 2 if i % 2 == 0 else ring - 1 - i // 2 for i in range(ring)]
    folded = [z * ring + y for z in range(2) for y in fold]
    return plain, folded if backward else folded[ring:] + folded[:ring]


def scan_kernel(backward, flags_ref, x_ref, out_ref):
    count = x_ref.shape[0]
    order = list(range(count))[:: -1 if backward else 1]
    even_order, odd_order = block_orders(count, backward)
    odd = lax.rem(lax.axis_index("head"), 2) == 1
    place = [jnp.where(odd, odd_order.index(b), even_order.index(b)) for b in range(count)]
    keep, take = (2, 3) if backward else (0, 1)
    running = jnp.zeros(x_ref.shape[1:], F32)
    out_ref[place[order[0]]] = running
    for b, later in zip(order[:-1], order[1:]):
        running = running * flags_ref[keep, b : b + 1] + x_ref[place[b]] * flags_ref[take, b : b + 1]
        out_ref[place[later]] = running


def masked_scores(q, k, ends):
    half = q.shape[0] // 2
    parts = []
    for start, size in ((0, half), (half, 2 * half)):
        token = lax.broadcasted_iota(I32, (half, size), 0) + start
        source = lax.broadcasted_iota(I32, (half, size), 1)
        allowed = (source <= token) & (token < ends[:, :size])
        parts.append(jnp.where(allowed, dot(q[start : start + half], k[:size], (1, 1)), 0.0).astype(BF16))
    return parts


def masked_turned(k, q, begins):
    half = q.shape[0] // 2
    parts = []
    for start, size in ((0, half), (half, 2 * half)):
        token = lax.broadcasted_iota(I32, (size, half), 1) + start
        source = lax.broadcasted_iota(I32, (size, half), 0)
        allowed = (source <= token) & (source >= begins[:, start : start + half])
        parts.append(jnp.where(allowed, dot(k[:size], q[start : start + half], (1, 1)), 0.0).astype(BF16))
    return parts


def intra_kernel(bounds_ref, edges_ref, flags_ref, q_ref, k_ref, v_ref, gain_ref, intra_ref, bounds_out_ref, flags_out_ref, gain_out_ref):
    half = q_ref.shape[0] // 2
    ends = edges_ref[4:5]
    bounds_out_ref[...] = bounds_ref[...]
    flags_out_ref[...] = flags_ref[...]
    gain_out_ref[...] = gain_ref[...]
    for cols in heads_of(q_ref):
        early, late = masked_scores(q_ref[:, cols], k_ref[:, cols], ends)
        intra_ref[:half, cols] = dot(early, v_ref[:half, cols], (1, 0))
        intra_ref[half:, cols] = dot(late, v_ref[:, cols], (1, 0))


def attend_kernel(bounds_ref, q_ref, intra_ref, prefix_ref, g_ref, gain_ref, attended_ref, sums_ref):
    rows = q_ref.shape[0]
    parts = rows // DH
    prefix = [prefix_ref[h].astype(BF16) for h in range(prefix_ref.shape[0])]
    for i in range(parts):
        part = slice(i * DH, (i + 1) * DH)
        from_head = row_index(DH) + i * DH < bounds_ref[0:1]
        squares = jnp.zeros((DH, DH), F32)
        crosses = jnp.zeros((DH, DH), F32)
        for h, cols in enumerate(heads_of(q_ref)):
            carried = dot(q_ref[part, cols], prefix[h], (1, 0))
            attended = intra_ref[part, cols] + jnp.where(from_head, carried, 0.0)
            attended_ref[part, cols] = attended
            squares += attended * attended
            crosses += attended * (gain_ref[:, cols] * g_ref[part, cols].astype(F32))
        square = jnp.sum(squares.T, axis=0, keepdims=True)
        cross = jnp.sum(crosses.T, axis=0, keepdims=True)
        for to in range(sums_ref.shape[0]):
            sums_ref[to, i : i + 1] = square
            sums_ref[to, parts + i : parts + i + 1] = cross


def grad_kernel(bounds_ref, q_ref, attended_ref, g_ref, gain_ref, sums_ref, normed_ref, state_ref):
    rows = attended_ref.shape[0]
    parts = rows // DH
    sums = jnp.sum(sums_ref[...], axis=0)
    inverse = lax.rsqrt(sums[:parts] / WIDTH + EPSILON)
    factor = inverse * inverse * inverse * (sums[parts:] / WIDTH)
    for i in range(parts):
        part = slice(i * DH, (i + 1) * DH)
        from_head = row_index(DH) + i * DH < bounds_ref[0:1]
        inverse_here = jnp.broadcast_to(inverse[i : i + 1], (DH, DH)).T
        factor_here = jnp.broadcast_to(factor[i : i + 1], (DH, DH)).T
        for h, cols in enumerate(heads_of(q_ref)):
            scaled = gain_ref[:, cols] * g_ref[part, cols].astype(F32)
            normed = (scaled * inverse_here - attended_ref[part, cols] * factor_here).astype(BF16)
            normed_ref[part, cols] = normed
            term = dot(jnp.where(from_head, q_ref[part, cols], jnp.zeros((), BF16)), normed, (0, 0))
            state_ref[h] = term if i == 0 else state_ref[h] + term


def products_kernel(
    bounds_ref, edges_ref, q_ref, k_ref, v_ref, normed_ref, prefix_ref, dq_ref, dk_ref, dv_ref
):
    rows = q_ref.shape[0]
    half = rows // 2
    from_head = row_index(rows) < bounds_ref[0:1]
    begins = edges_ref[0:1]
    for h, cols in enumerate(heads_of(q_ref)):
        q, k, normed = q_ref[:, cols], k_ref[:, cols], normed_ref[:, cols]
        early, late = masked_turned(k, q, begins)
        upper = dot(late, normed[half:], (1, 0))
        dv_ref[:half, cols] = (upper[:half] + dot(early, normed[:half], (1, 0))).astype(BF16)
        dv_ref[half:, cols] = upper[half:].astype(BF16)
        early, late = masked_turned(v_ref[:, cols], normed, begins)
        upper = dot(late, q[half:], (1, 0))
        dk_ref[:half, cols] = (upper[:half] + dot(early, q[:half], (1, 0))).astype(BF16)
        dk_ref[half:, cols] = upper[half:].astype(BF16)
        carried = dot(normed, prefix_ref[h].astype(BF16), (1, 1))
        carried = jnp.where(from_head, carried, 0.0)
        dq_ref[:half, cols] = (dot(early, k[:half], (0, 0)) + carried[:half]).astype(BF16)
        dq_ref[half:, cols] = (dot(late, k, (0, 0)) + carried[half:]).astype(BF16)


def final_kernel(bounds_ref, k_ref, v_ref, dk_ref, dv_ref, later_ref, key_hbm, value_hbm, key_buf, value_buf, sems):
    rows = k_ref.shape[0]
    to_tail = row_index(rows) >= bounds_ref[4:5]
    stores = []
    for h, cols in enumerate(heads_of(k_ref)):
        later = later_ref[h].astype(BF16)
        dk = dot(v_ref[:, cols], later, (1, 1))
        key_buf[:, cols] = (dk_ref[:, cols] + jnp.where(to_tail, dk, 0.0)).astype(BF16)
        stores.append(pltpu.make_async_copy(key_buf.at[:, cols], key_hbm.at[:, cols], sems.at[2 * h]))
        stores[-1].start()
        dv = dot(k_ref[:, cols], later, (1, 0))
        value_buf[:, cols] = (dv_ref[:, cols] + jnp.where(to_tail, dv, 0.0)).astype(BF16)
        stores.append(pltpu.make_async_copy(value_buf.at[:, cols], value_hbm.at[:, cols], sems.at[2 * h + 1]))
        stores[-1].start()
    for store in stores:
        store.wait()


HBM = pl.BlockSpec(memory_space=pltpu.HBM)
VMEM = pl.BlockSpec(memory_space=pltpu.VMEM)


def call(kernel, arrays, outs, flops, name, in_specs=None, out_specs=None, scratch=(), room=16):
    out_shape = tuple(jax.ShapeDtypeStruct(s, d) for s, d in outs)
    moved = sum(a.size * a.dtype.itemsize for a in arrays) + sum(o.size * o.dtype.itemsize for o in out_shape)
    return pl.pallas_call(
        kernel,
        out_shape=out_shape,
        in_specs=in_specs or [VMEM] * len(arrays),
        out_specs=out_specs or (VMEM,) * len(outs),
        scratch_shapes=list(scratch),
        compiler_params=pltpu.CompilerParams(vmem_limit_bytes=int(room * 1024 * 1024)),
        cost_estimate=pl.CostEstimate(flops=flops, bytes_accessed=moved, transcendentals=0),
        name=name,
    )(*arrays)


def on_device(queries, keys, values, out_grad, gain, doc_starts):
    rows, width = queries.shape
    heads = width // DH
    per = lax.axis_size("seq") // QUARTERS
    head_devices = lax.axis_size("head")
    gain_row = gain.reshape(1, width)
    all_groups = []
    for backward in (False, True):
        orders = block_orders(per, backward)
        all_groups.append(
            [[(g * per + b) * head_devices + m for b in orders[m % 2]] for g in range(QUARTERS) for m in range(head_devices)]
        )
    state_shape = (heads, DH, DH)
    pieces = (per, heads * DH // per, DH)
    state_flops = 2 * rows * width * DH
    full_flops = 2 * rows * rows * width
    whole = (rows, width)

    def swap(x, backward):
        groups = all_groups[backward]
        return lax.all_to_all(x.reshape(pieces), ("seq", "head"), 0, 0, axis_index_groups=groups, tiled=True)

    def scan(state, flags, backward):
        (mine,) = call(functools.partial(scan_kernel, backward), (flags, swap(state, backward)), [(pieces, F32)], 0, "state_scan")
        return swap(mine, backward).reshape(state_shape)

    kv_state, bounds, edges, flags = call(
        functools.partial(kv_kernel, per),
        (doc_starts, keys, values),
        [(state_shape, F32), ((8, DH), I32), ((8, rows), I32), ((4, per, DH), F32)],
        state_flops,
        "kv_state",
        in_specs=[HBM] * 3,
        room=60,
        scratch=[
            pltpu.SMEM(doc_starts.shape, I32),
            pltpu.VMEM(whole, BF16),
            pltpu.VMEM(whole, BF16),
            pltpu.SemaphoreType.DMA((1 + 2 * LOADS,)),
        ],
    )
    intra, bounds, flags, gain_row = call(
        intra_kernel,
        (bounds, edges, flags, queries, keys, values, gain_row),
        [(whole, F32), (bounds.shape, I32), (flags.shape, F32), (gain_row.shape, F32)],
        2 * full_flops,
        "intra",
    )
    prefix = scan(kv_state, flags, False)
    attended, sums = call(
        attend_kernel,
        (bounds, queries, intra, prefix, out_grad, gain_row),
        [(whole, F32), ((head_devices, 2 * rows // DH, DH), F32)],
        state_flops,
        "attend",
    )
    sums = lax.all_to_all(sums, "head", 0, 0, tiled=True)
    normed, grad_state = call(
        grad_kernel,
        (bounds, queries, attended, out_grad, gain_row, sums),
        [(whole, BF16), (state_shape, F32)],
        state_flops,
        "normed_grad",
    )
    later = scan(grad_state, flags, True)
    query_grad, key_part, value_part = call(
        products_kernel,
        (bounds, edges, queries, keys, values, normed, prefix),
        [(whole, BF16), (whole, BF16), (whole, BF16)],
        5 * full_flops + state_flops,
        "products",
    )
    key_grad, value_grad = call(
        final_kernel,
        (bounds, keys, values, key_part, value_part, later),
        [(whole, BF16), (whole, BF16)],
        2 * state_flops,
        "key_value_grad",
        out_specs=(HBM, HBM),
        scratch=[
            pltpu.VMEM(whole, BF16),
            pltpu.VMEM(whole, BF16),
            pltpu.SemaphoreType.DMA((2 * heads,)),
        ],
    )
    return query_grad, key_grad, value_grad


def solution(mesh):
    placed = (P("seq", "head"),) * 4 + (P("head"), P())
    return jax.shard_map(
        on_device,
        mesh=mesh,
        in_specs=placed,
        out_specs=(P("seq", "head"),) * 3,
        check_vma=False,
    )
```
